32 devices in a mesh: groups: 2 (over y), seq: 4 (over z), head: 2 (over x), rep: 2 (over core).
Axes of the slice: x: 2, y: 2, z: 4, core: 2. Of those that a mesh axis runs over, the one named last changes fastest.
Arguments:
- queries: bfloat16 [8192, 2048], P(('groups', 'seq'), ('head', 'rep')), parts along dimension 0, may hold values from -8 to 8
- keys_values: bfloat16 [2, 8192, 2048], P(None, ('groups', 'seq'), ('head', 'rep')), parts along dimension 1, may hold values from -8 to 8
- pack_pos: int32 [1024], P('groups'), parts along dimension 0, may hold values from 0 to 4095
- bounds: int32 [2, 8192], P(None, ('groups', 'seq')), parts along dimension 1, may hold values from 0 to 4096, as said below
- radius: int32 [32], P(('head', 'rep')), may hold values from 128 to 512, as said below
- pack_proj: bfloat16 [2, 2048, 2048], P(None, None, ('head', 'rep')), may hold values from -0.5 to 0.5
Outputs:
- mixed: bfloat16 [8192, 2048], P(('groups', 'seq'), ('head', 'rep')), parts along dimension 0
The draws below stay inside these ranges and needn't reach their ends.
There are 2 independent parts, one for each index of `groups`. The reference program is written for one: setup_inputs(seed, part) draws one part's arguments, and reference() takes and returns one part's arrays. A program takes and returns all parts, laid end to end along the dimension named above; an argument that names none is the same for every part. Nothing has to cross between parts.
Inputs may be any that keep to these rules, and one draw needn't show every extreme that they name: bounds[0, s] and bounds[1, s] are the first position and the end (exclusive) of the document of token s; the 8 documents are contiguous and tile the sequence. Some head has radius exactly 512.
All inputs are finite; a program needn't handle non-finite values.
Results may differ from the reference program's by a relative error of at most 0.012.
Values may be sent and summed in bfloat16 or wider, within the bound.
A program may use at most 128 MiB of HBM per device.

```python
import math
import jax
import jax.numpy as jnp
from jax import lax

HEADS = 32
HEAD_DIM = 64
D = 2048
PACK = 512
RADIUS = 512
TOK_DEV = 1024
SEQ_LEN = 4096
DOCS = 8


def draw_queries(key, part):
    own_key = jax.random.fold_in(key, 11)
    values = jnp.clip(2.0 * jax.random.normal(own_key, (SEQ_LEN, D), jnp.float32), -8.0, 8.0)
    return values.astype(jnp.bfloat16)


def draw_keys_values(key, part):
    own_key = jax.random.fold_in(key, 23)
    values = jnp.clip(jax.random.normal(own_key, (2, SEQ_LEN, D), jnp.float32), -6.0, 6.0)
    return values.astype(jnp.bfloat16)


def draw_bounds(key, part):
    own_key = jax.random.fold_in(key, 7101)
    cuts = jnp.sort(jax.random.permutation(own_key, SEQ_LEN - 1)[:DOCS - 1] + 1).astype(jnp.int32)
    edges = jnp.concatenate([jnp.zeros((1,), jnp.int32), cuts, jnp.full((1,), SEQ_LEN, jnp.int32)])
    position = jnp.arange(SEQ_LEN, dtype=jnp.int32)
    which_doc = (jnp.searchsorted(edges, position, side='right') - 1).astype(jnp.int32)
    starts = edges[which_doc]
    ends = edges[which_doc + 1]
    return jnp.stack([starts, ends]).astype(jnp.int32)


def draw_radius(key, part):
    own_key = jax.random.fold_in(key, 7201)
    draw_key, pick_key = jax.random.split(own_key)
    widths = jax.random.randint(draw_key, (HEADS,), RADIUS // 4, RADIUS + 1)
    widest = jax.random.randint(pick_key, (), 0, HEADS)
    return jnp.where(jnp.arange(HEADS) == widest, RADIUS, widths).astype(jnp.int32)


def touch_ends(drawn, rng, least, largest):
    longest = drawn.shape.index(max(drawn.shape))
    spots = []
    for shift in (0, 1):
        where = [jax.random.randint(jax.random.fold_in(rng, axis), (), 0, length) for axis, length in enumerate(drawn.shape)]
        where[longest] = (where[longest] + shift) % drawn.shape[longest]
        spots.append(tuple(where))
    return drawn.at[spots[0]].set(least).at[spots[1]].set(largest)


def levels(stream_key, shape, pieces, low, top_value):
    loudness = 1.0
    for dim, parts in pieces:
        draws = jax.random.uniform(jax.random.fold_in(jax.random.fold_in(stream_key, 6), dim), (parts,), jnp.float32, low / len(pieces), top_value / len(pieces))
        loudness = loudness * jnp.repeat(jnp.exp(draws), shape[dim] // parts).reshape((-1,) + (1,) * (len(shape) - 1 - dim))
    return loudness


def centred(key, shape, spread, bound, cuts=(), held_as=jnp.bfloat16):
    level = levels(key, shape, cuts, -0.22, 0.18) if cuts else 1.0
    entries = jax.random.normal(key, shape, jnp.float32) * spread * level
    return jnp.minimum(jnp.maximum(entries, -bound), bound).astype(held_as)


def setup_inputs(seed: int = 0, part: int = 0) -> dict:
    key_of = jax.random.split(jax.random.key(seed), 7)
    part_keys = jax.random.split(jax.random.fold_in(key_of[6], part), 7)
    queries = draw_queries(jax.random.fold_in(jax.random.fold_in(key_of[6], part), 71), part)
    keys_values = draw_keys_values(jax.random.fold_in(jax.random.fold_in(key_of[6], part), 71), part)
    pack_pos = touch_ends(jax.random.randint(part_keys[2], (PACK,), 0, SEQ_LEN), jax.random.fold_in(part_keys[2], 1), 0, SEQ_LEN - 1).astype(jnp.int32)
    bounds = draw_bounds(jax.random.fold_in(jax.random.fold_in(key_of[6], part), 71), part)
    radius = draw_radius(jax.random.fold_in(key_of[6], 71), part)
    pack_proj = centred(key_of[5], (2, D, D), (D // 16) ** -0.5, 0.5, ((2, 4),))
    return {"queries": queries, "keys_values": keys_values, "pack_pos": pack_pos, "bounds": bounds, "radius": radius, "pack_proj": pack_proj}


def pack_head(pack_query, keys_values, head_number):
    column = (head_number * HEAD_DIM).astype(jnp.int32)
    scale = 1.0 / math.sqrt(HEAD_DIM)
    query_head = lax.dynamic_slice_in_dim(pack_query, column, HEAD_DIM, 1)
    key_head = lax.dynamic_slice_in_dim(keys_values[0], column, HEAD_DIM, 1)
    value_head = lax.dynamic_slice_in_dim(keys_values[1], column, HEAD_DIM, 1)
    scores = jnp.dot(query_head, key_head.T, preferred_element_type=jnp.float32) * scale
    highest = lax.optimization_barrier(jnp.max(scores, axis=1, keepdims=True))
    weights = jnp.exp(scores - highest)
    totals = lax.optimization_barrier(jnp.sum(weights, axis=1, keepdims=True))
    summed = jnp.dot(weights.astype(jnp.bfloat16), value_head, preferred_element_type=jnp.float32)
    return summed / totals

def attend(query_block, window_keys, window_values, pack_key_heads, pack_value_heads, lower, upper, radius, first_pos):
    rows_here = query_block.shape[0]
    window_len = window_keys.shape[0]
    scale = 1.0 / math.sqrt(HEAD_DIM)
    pack_scores = jnp.einsum('qhd,phd->hqp', query_block, pack_key_heads) * scale
    window_scores = jnp.einsum('qhd,khd->hqk', query_block, window_keys) * scale
    query_pos = first_pos + jnp.arange(rows_here, dtype=jnp.int32)
    key_pos = first_pos - RADIUS + jnp.arange(window_len, dtype=jnp.int32)
    distance = jnp.abs(key_pos[None, :] - query_pos[:, None])
    inside = (key_pos[None, :] >= lower[:, None]) & (key_pos[None, :] < upper[:, None])
    allowed = (distance[None, :, :] <= radius[:, None, None]) & inside[None, :, :]
    window_scores = jnp.where(allowed, window_scores, -1e+30)
    highest = jnp.maximum(lax.optimization_barrier(jnp.max(pack_scores, axis=2)), lax.optimization_barrier(jnp.max(window_scores, axis=2)))
    pack_weights = jnp.exp(pack_scores - highest[:, :, None])
    window_weights = jnp.exp(window_scores - highest[:, :, None])
    totals = lax.optimization_barrier(jnp.sum(pack_weights, axis=2)) + lax.optimization_barrier(jnp.sum(window_weights, axis=2))
    pack_rounded = lax.optimization_barrier(pack_weights.astype(jnp.bfloat16)).astype(jnp.float32)
    window_rounded = lax.optimization_barrier(window_weights.astype(jnp.bfloat16)).astype(jnp.float32)
    summed = jnp.einsum('hqp,phd->qhd', pack_rounded, pack_value_heads) + jnp.einsum('hqk,khd->qhd', window_rounded, window_values)
    return (summed / totals.T[:, :, None]).reshape(rows_here, -1).astype(jnp.bfloat16)

def reference(queries, keys_values, pack_pos, bounds, radius, pack_proj):
    seq_total = queries.shape[0]
    width = queries.shape[1]
    pack_query = jnp.take(queries, pack_pos, axis=0)
    heads_out = lax.map(lambda head_number: pack_head(pack_query, keys_values, head_number), jnp.arange(HEADS, dtype=jnp.int32))
    packed = jnp.transpose(heads_out, (1, 0, 2)).reshape(PACK, width).astype(jnp.bfloat16)
    pack_keys = jnp.dot(packed, pack_proj[0], preferred_element_type=jnp.float32).astype(jnp.bfloat16)
    pack_values = jnp.dot(packed, pack_proj[1], preferred_element_type=jnp.float32).astype(jnp.bfloat16)
    rows_per = math.gcd(TOK_DEV, 512)
    window_len = rows_per + 2 * RADIUS
    padded = jnp.pad(keys_values, ((0, 0), (RADIUS, RADIUS), (0, 0)))
    pack_key_heads = pack_keys.astype(jnp.float32).reshape(PACK, HEADS, HEAD_DIM)
    pack_value_heads = pack_values.astype(jnp.float32).reshape(PACK, HEADS, HEAD_DIM)

    def token_block(which_block):
        offset_row = (which_block * rows_per).astype(jnp.int32)
        query_block = lax.dynamic_slice_in_dim(queries, offset_row, rows_per, 0).astype(jnp.float32).reshape(rows_per, HEADS, HEAD_DIM)
        window = lax.dynamic_slice_in_dim(padded, offset_row, window_len, 1).astype(jnp.float32)
        window_keys = window[0].reshape(window_len, HEADS, HEAD_DIM)
        window_values = window[1].reshape(window_len, HEADS, HEAD_DIM)
        lower = lax.dynamic_slice_in_dim(bounds[0], offset_row, rows_per, 0)
        upper = lax.dynamic_slice_in_dim(bounds[1], offset_row, rows_per, 0)
        return attend(query_block, window_keys, window_values, pack_key_heads, pack_value_heads, lower, upper, radius, offset_row)
    blocks_out = lax.map(token_block, jnp.arange(seq_total // rows_per, dtype=jnp.int32))
    return blocks_out.reshape(seq_total, width)
```

```python
import functools
import math

import jax
import jax.numpy as jnp
from jax import lax
from jax.experimental import pallas as pl
from jax.experimental.pallas import tpu as pltpu
from jax.sharding import PartitionSpec as P

HEAD_DIM = 64
PACK = 512
RADIUS = 512
PAIR = 2 * HEAD_DIM
ROWS = 256
LOG2E = 1.4426950408889634
FACTOR = LOG2E / math.sqrt(HEAD_DIM)
LOW = -1e30
VMEM = 48 * 1024 * 1024


def lane_half(rows):
    return lax.broadcasted_iota(jnp.int32, (rows, PAIR), 1) // HEAD_DIM


def dot_t(a, b):
    return lax.dot_general(a, b, (((1,), (1,)), ((), ())), preferred_element_type=jnp.float32)


def only_head(x, h):
    return jnp.where(lane_half(x.shape[0]) == h, x, jnp.zeros_like(x))


def with_ones(x, h):
    return jnp.where(lane_half(x.shape[0]) == h, x, jnp.ones_like(x))


def softmax_dot(scores, values):
    top = jnp.max(scores, axis=1, keepdims=True)
    weights = jnp.exp2((scores - top) * FACTOR)
    acc = jnp.dot(weights.astype(jnp.bfloat16), values, preferred_element_type=jnp.float32)
    return top * FACTOR, acc


def merge_heads(tops, accs):
    half = lane_half(accs[0].shape[0])
    summed = jnp.where(half == 0, accs[0], accs[1])
    total = pltpu.roll(jnp.where(half == 0, accs[1], accs[0]), HEAD_DIM, 1)
    top = jnp.where(half == 0, tops[0], tops[1])
    return summed, total, top


def pack_kernel(q_ref, kv_ref, out_ref, lse_ref):
    keys = kv_ref[0]
    values = [with_ones(kv_ref[1], h) for h in range(2)]
    for r in range(0, q_ref.shape[0], ROWS):
        rows = pl.ds(r, ROWS)
        q = q_ref[rows, :]
        tops, accs = [], []
        for h in range(2):
            top, acc = softmax_dot(dot_t(only_head(q, h), keys), values[h])
            tops.append(top)
            accs.append(acc)
        summed, total, top = merge_heads(tops, accs)
        out_ref[rows, :] = (summed / total).astype(jnp.bfloat16)
        lse_ref[rows, :] = top + jnp.log2(total)


def pack_attention(pack_query, keys_values):
    rows, width = pack_query.shape
    tokens = keys_values.shape[1]
    return pl.pallas_call(
        pack_kernel,
        grid=(width // PAIR,),
        in_specs=[
            pl.BlockSpec((rows, PAIR), lambda i: (0, i)),
            pl.BlockSpec((2, tokens, PAIR), lambda i: (0, 0, i)),
        ],
        out_specs=[pl.BlockSpec((rows, PAIR), lambda i: (0, i))] * 2,
        out_shape=[
            jax.ShapeDtypeStruct((rows, width), jnp.bfloat16),
            jax.ShapeDtypeStruct((rows, width), jnp.float32),
        ],
        compiler_params=pltpu.CompilerParams(vmem_limit_bytes=VMEM),
        cost_estimate=pl.CostEstimate(
            flops=16 * rows * tokens * width,
            bytes_accessed=4 * tokens * width + 8 * rows * width,
            transcendentals=rows * tokens * width // HEAD_DIM,
        ),
        name="pack_attention",
    )(pack_query, keys_values)


def window_kernel(
    radius_ref, bounds_ref, q_ref, own_ref, left_ref, right_ref, limits_ref,
    out_ref, lse_ref, keys, values, accs, tops,
):
    tokens = q_ref.shape[0]
    pair = pl.program_id(0)
    for at, ref in ((0, left_ref), (RADIUS, own_ref), (RADIUS + tokens, right_ref)):
        span = pl.ds(at, ref.shape[1])
        keys[span, :] = ref[0]
        for h in range(2):
            values[h, span, :] = with_ones(ref[1], h)

    def block(b, carry):
        first = pl.multiple_of(b * ROWS, ROWS)
        rows = pl.ds(first, ROWS)
        q = q_ref[rows, :]
        position = first + RADIUS + lax.broadcasted_iota(jnp.int32, (ROWS, 1), 0)
        lower = limits_ref[rows, 0:1]
        upper = limits_ref[rows, 1:2]
        for h in range(2):
            radius = radius_ref[2 * pair + h]
            low = jnp.maximum(lower, position - radius)
            high = jnp.minimum(upper, position + radius + 1)
            start = jnp.maximum(bounds_ref[first], first + RADIUS - radius)
            start = jnp.maximum(start, 0) // 128 * 128
            end = jnp.minimum(bounds_ref[tokens + first + ROWS - 1], first + RADIUS + ROWS + radius)
            need = end - start
            masked_q = only_head(q, h)

            def body(width):
                at = pl.multiple_of(jnp.minimum(start, tokens + 2 * RADIUS - width), 128)
                scores = dot_t(masked_q, keys[pl.ds(at, width), :])
                spot = lax.broadcasted_iota(jnp.int32, (ROWS, width), 1)
                allowed = (spot >= low - at) & (spot < high - at)
                top, acc = softmax_dot(
                    jnp.where(allowed, scores, LOW), values[h, pl.ds(at, width), :]
                )
                accs[h] = acc
                tops[h] = jnp.broadcast_to(top, (ROWS, PAIR))

            widest = ROWS + 2 * RADIUS
            widths = [w for w in (512, 640, 768, 896, 1024, 1152) if w < widest] + [widest]
            for index, width in enumerate(widths):
                fits = need <= width if width < widest else need > widths[index - 1]
                if 0 < index and width < widest:
                    fits = fits & (need > widths[index - 1])
                pl.when(fits)(functools.partial(body, width))
        summed, total, top = merge_heads([tops[0], tops[1]], [accs[0], accs[1]])
        out_ref[rows, :] = summed / total
        lse_ref[rows, :] = top + jnp.log2(total)
        return carry

    lax.fori_loop(0, tokens // ROWS, block, 0)


def window_attention(queries, keys_values, left, right, bounds, radius, first_pos):
    tokens, width = queries.shape
    limits = bounds - (first_pos - RADIUS)
    cost = tokens * (ROWS + 2 * RADIUS)
    spec = lambda shape: pl.BlockSpec(shape, lambda i, *_: (0,) * (len(shape) - 1) + (i,))
    return pl.pallas_call(
        window_kernel,
        grid_spec=pltpu.PrefetchScalarGridSpec(
            num_scalar_prefetch=2,
            grid=(width // PAIR,),
            in_specs=[
                spec((tokens, PAIR)),
                spec((2, tokens, PAIR)),
                spec((2, RADIUS, PAIR)),
                spec((2, RADIUS, PAIR)),
                pl.BlockSpec((tokens, 2), lambda i, *_: (0, 0)),
            ],
            out_specs=[spec((tokens, PAIR))] * 2,
            scratch_shapes=[
                pltpu.VMEM((tokens + 2 * RADIUS, PAIR), jnp.bfloat16),
                pltpu.VMEM((2, tokens + 2 * RADIUS, PAIR), jnp.bfloat16),
                pltpu.VMEM((2, ROWS, PAIR), jnp.float32),
                pltpu.VMEM((2, ROWS, PAIR), jnp.float32),
            ],
        ),
        out_shape=[jax.ShapeDtypeStruct((tokens, width), jnp.float32)] * 2,
        compiler_params=pltpu.CompilerParams(vmem_limit_bytes=VMEM),
        cost_estimate=pl.CostEstimate(
            flops=16 * cost * width,
            bytes_accessed=20 * tokens * width,
            transcendentals=cost * width // HEAD_DIM,
        ),
        name="window_attention",
    )(radius, limits.reshape(-1), queries, keys_values, left, right, limits.T)


def final_kernel(q_ref, pack_ref, part_ref, lse_ref, out_ref):
    keys = pack_ref[0]
    values = [with_ones(pack_ref[1], h) for h in range(2)]
    for r in range(0, q_ref.shape[0], ROWS):
        rows = pl.ds(r, ROWS)
        q = q_ref[rows, :]
        tops, accs = [], []
        for h in range(2):
            top, acc = softmax_dot(dot_t(only_head(q, h), keys), values[h])
            tops.append(top)
            accs.append(acc)
        summed, total, top = merge_heads(tops, accs)
        other = lse_ref[rows, :]
        highest = jnp.maximum(top, other)
        mine = jnp.exp2(top - highest)
        theirs = jnp.exp2(other - highest)
        out_ref[rows, :] = (
            (summed * mine + part_ref[rows, :] * theirs) / (total * mine + theirs)
        ).astype(jnp.bfloat16)


def final_attention(queries, pack_kv, part, lse):
    tokens, width = queries.shape
    spec = pl.BlockSpec((tokens, PAIR), lambda i: (0, i))
    return pl.pallas_call(
        final_kernel,
        grid=(width // PAIR,),
        in_specs=[spec, pl.BlockSpec((2, PACK, PAIR), lambda i: (0, 0, i)), spec, spec],
        out_specs=spec,
        out_shape=jax.ShapeDtypeStruct((tokens, width), jnp.bfloat16),
        compiler_params=pltpu.CompilerParams(vmem_limit_bytes=VMEM),
        cost_estimate=pl.CostEstimate(
            flops=16 * tokens * PACK * width,
            bytes_accessed=12 * tokens * width,
            transcendentals=tokens * PACK * width // HEAD_DIM,
        ),
        name="final_attention",
    )(queries, pack_kv, part, lse)


def project_kernel(order_ref, part_ref, proj_ref, out_ref, acc):
    step = pl.program_id(0)

    @pl.when(step == 0)
    def _():
        acc[...] = jnp.zeros_like(acc)

    for which in range(2):
        acc[which] += jnp.dot(part_ref[0], proj_ref[which], preferred_element_type=jnp.float32)

    @pl.when(step == pl.num_programs(0) - 1)
    def _():
        out_ref[...] = acc[...].astype(jnp.bfloat16)


def project(order, parts, pack_proj):
    count, rows, width = parts.shape
    columns = pack_proj.shape[2]
    return pl.pallas_call(
        project_kernel,
        grid_spec=pltpu.PrefetchScalarGridSpec(
            num_scalar_prefetch=1,
            grid=(count,),
            in_specs=[
                pl.BlockSpec((1, rows, width), lambda i, order: (i, 0, 0)),
                pl.BlockSpec((2, width, columns), lambda i, order: (0, order[i], 0)),
            ],
            out_specs=pl.BlockSpec((2, rows, columns), lambda i, order: (0, 0, 0)),
            scratch_shapes=[pltpu.VMEM((2, rows, columns), jnp.float32)],
        ),
        out_shape=jax.ShapeDtypeStruct((2, rows, columns), jnp.bfloat16),
        compiler_params=pltpu.CompilerParams(vmem_limit_bytes=VMEM),
        name="project",
    )(order, parts, pack_proj)


def shifted(x, axis, count, shift):
    return lax.ppermute(x, axis, [(i, (i + shift) % count) for i in range(count)])


def shards(queries, keys_values, pack_pos, bounds, radius, pack_proj):
    tokens, width = queries.shape
    heads = radius.shape[0]
    count = lax.axis_size("seq")
    share = PACK // count
    me = lax.axis_index("seq")
    first_pos = me * tokens

    ahead = (me + jnp.arange(count, dtype=jnp.int32)) % count
    local = pack_pos.reshape(count, share)[ahead].reshape(-1) - first_pos
    selector = (local[:, None] == jnp.arange(tokens, dtype=jnp.int32)[None, :]).astype(jnp.bfloat16)
    picked = jnp.dot(selector, queries, preferred_element_type=jnp.float32).astype(jnp.bfloat16)
    picked = picked.reshape(count, share, width)
    mine = picked[0]
    for s in range(1, count):
        mine = mine + shifted(picked[s], "seq", count, s)
    pack_query = jnp.concatenate([mine] + [shifted(mine, "seq", count, s) for s in range(1, count)])

    ends = count - 1
    left = lax.ppermute(
        keys_values[:, tokens - RADIUS :], "seq", [(i, i + 1) for i in range(ends)]
    )
    right = lax.ppermute(keys_values[:, :RADIUS], "seq", [(i + 1, i) for i in range(ends)])

    part, lse = pack_attention(pack_query, keys_values)
    part = part.reshape(count, share, width)
    lse = lse[:, ::HEAD_DIM].reshape(count, share, heads)
    parts, lses = [part[0]], [lse[0]]
    for s in range(1, count):
        parts.append(shifted(part[count - s], "seq", count, s))
        lses.append(shifted(lse[count - s], "seq", count, s))
    lses = jnp.stack(lses)
    weights = jnp.exp2(lses - jnp.max(lses, axis=0, keepdims=True))
    weights = weights / jnp.sum(weights, axis=0, keepdims=True)
    packed = sum(
        parts[j].astype(jnp.float32).reshape(share, heads, HEAD_DIM) * weights[j][:, :, None]
        for j in range(count)
    )
    packed = packed.reshape(share, width).astype(jnp.bfloat16)

    axes = ("head", "rep")
    sides = lax.axis_size("head") * lax.axis_size("rep")
    here = lax.axis_index("head") * lax.axis_size("rep") + lax.axis_index("rep")
    gathered = jnp.stack([packed] + [shifted(packed, axes, sides, s) for s in range(1, sides)])
    order = (here - jnp.arange(sides, dtype=jnp.int32)) % sides
    pack_share = project(order, gathered, pack_proj)
    pack_kv = jnp.concatenate(
        [pack_share] + [shifted(pack_share, "seq", count, s) for s in range(1, count)], axis=1
    )
    window, window_lse = window_attention(
        queries, keys_values, left, right, bounds, radius, first_pos
    )
    return final_attention(queries, pack_kv, window, window_lse)


def solution(mesh):
    return jax.shard_map(
        shards,
        mesh=mesh,
        in_specs=(
            P(("groups", "seq"), ("head", "rep")),
            P(None, ("groups", "seq"), ("head", "rep")),
            P("groups"),
            P(None, ("groups", "seq")),
            P(("head", "rep")),
            P(None, None, ("head", "rep")),
        ),
        out_specs=P(("groups", "seq"), ("head", "rep")),
        check_vma=False,
    )
```

```python
import functools
import math

import jax
import jax.numpy as jnp
from jax import lax
from jax.experimental import pallas as pl
from jax.experimental.pallas import tpu as pltpu
from jax.sharding import PartitionSpec as P

HEAD_DIM = 64
PACK = 512
RADIUS = 512
PAIR = 2 * HEAD_DIM
ROWS = 256
LOG2E = 1.4426950408889634
FACTOR = LOG2E / math.sqrt(HEAD_DIM)
LOW = -1e30
VMEM = 48 * 1024 * 1024


def lane_half(rows):
    return lax.broadcasted_iota(jnp.int32, (rows, PAIR), 1) // HEAD_DIM


def dot_t(a, b):
    return lax.dot_general(a, b, (((1,), (1,)), ((), ())), preferred_element_type=jnp.float32)


def only_head(x, h):
    return jnp.where(lane_half(x.shape[0]) == h, x, jnp.zeros_like(x))


def with_ones(x, h):
    return jnp.where(lane_half(x.shape[0]) == h, x, jnp.ones_like(x))


def softmax_dot(scores, values):
    top = jnp.max(scores, axis=1, keepdims=True)
    weights = jnp.exp2((scores - top) * FACTOR)
    acc = jnp.dot(weights.astype(jnp.bfloat16), values, preferred_element_type=jnp.float32)
    return top * FACTOR, acc


def merge_heads(tops, accs):
    half = lane_half(accs[0].shape[0])
    summed = jnp.where(half == 0, accs[0], accs[1])
    total = pltpu.roll(jnp.where(half == 0, accs[1], accs[0]), HEAD_DIM, 1)
    top = jnp.where(half == 0, tops[0], tops[1])
    return summed, total, top


def pack_kernel(q_ref, kv_ref, out_ref, lse_ref):
    keys = kv_ref[0]
    values = [with_ones(kv_ref[1], h) for h in range(2)]
    for r in range(0, q_ref.shape[0], ROWS):
        rows = pl.ds(r, ROWS)
        q = q_ref[rows, :]
        tops, accs = [], []
        for h in range(2):
            top, acc = softmax_dot(dot_t(only_head(q, h), keys), values[h])
            tops.append(top)
            accs.append(acc)
        summed, total, top = merge_heads(tops, accs)
        out_ref[rows, :] = (summed / total).astype(jnp.bfloat16)
        lse_ref[rows, :] = top + jnp.log2(total)


def pack_attention(pack_query, keys_values):
    rows, width = pack_query.shape
    tokens = keys_values.shape[1]
    return pl.pallas_call(
        pack_kernel,
        grid=(width // PAIR,),
        in_specs=[
            pl.BlockSpec((rows, PAIR), lambda i: (0, i)),
            pl.BlockSpec((2, tokens, PAIR), lambda i: (0, 0, i)),
        ],
        out_specs=[pl.BlockSpec((rows, PAIR), lambda i: (0, i))] * 2,
        out_shape=[
            jax.ShapeDtypeStruct((rows, width), jnp.bfloat16),
            jax.ShapeDtypeStruct((rows, width), jnp.float32),
        ],
        compiler_params=pltpu.CompilerParams(vmem_limit_bytes=VMEM),
        cost_estimate=pl.CostEstimate(
            flops=16 * rows * tokens * width,
            bytes_accessed=4 * tokens * width + 8 * rows * width,
            transcendentals=rows * tokens * width // HEAD_DIM,
        ),
        name="pack_attention",
    )(pack_query, keys_values)


def window_kernel(
    first_pair, radius_ref, bounds_ref, q_ref, own_ref, left_ref, right_ref, limits_ref, *rest
):
    out_ref, lse_ref, keys, values, accs, tops = rest[-6:]
    tokens = q_ref.shape[0]
    pair = first_pair + pl.program_id(0)
    for at, ref in ((0, left_ref), (RADIUS, own_ref), (RADIUS + tokens, right_ref)):
        span = pl.ds(at, ref.shape[1])
        keys[span, :] = ref[0]
        for h in range(2):
            values[h, span, :] = with_ones(ref[1], h)

    def block(b, carry):
        first = pl.multiple_of(b * ROWS, ROWS)
        rows = pl.ds(first, ROWS)
        q = q_ref[rows, :]
        position = first + RADIUS + lax.broadcasted_iota(jnp.int32, (ROWS, 1), 0)
        lower = limits_ref[rows, 0:1]
        upper = limits_ref[rows, 1:2]
        for h in range(2):
            radius = radius_ref[2 * pair + h]
            low = jnp.maximum(lower, position - radius)
            high = jnp.minimum(upper, position + radius + 1)
            start = jnp.maximum(bounds_ref[first], first + RADIUS - radius)
            start = jnp.maximum(start, 0) // 128 * 128
            end = jnp.minimum(bounds_ref[tokens + first + ROWS - 1], first + RADIUS + ROWS + radius)
            need = end - start
            masked_q = only_head(q, h)

            def body(width):
                at = pl.multiple_of(jnp.minimum(start, tokens + 2 * RADIUS - width), 128)
                scores = dot_t(masked_q, keys[pl.ds(at, width), :])
                spot = lax.broadcasted_iota(jnp.int32, (ROWS, width), 1)
                allowed = (spot >= low - at) & (spot < high - at)
                top, acc = softmax_dot(
                    jnp.where(allowed, scores, LOW), values[h, pl.ds(at, width), :]
                )
                accs[h] = acc
                tops[h] = jnp.broadcast_to(top, (ROWS, PAIR))

            widest = ROWS + 2 * RADIUS
            widths = [w for w in (512, 640, 768, 896, 1024, 1152) if w < widest] + [widest]
            for index, width in enumerate(widths):
                fits = need <= width if width < widest else need > widths[index - 1]
                if 0 < index and width < widest:
                    fits = fits & (need > widths[index - 1])
                pl.when(fits)(functools.partial(body, width))
        summed, total, top = merge_heads([tops[0], tops[1]], [accs[0], accs[1]])
        out_ref[rows, :] = summed / total
        lse_ref[rows, :] = top + jnp.log2(total)
        return carry

    lax.fori_loop(0, tokens // ROWS, block, 0)


def window_attention(queries, keys_values, left, right, limits, radius, pairs, done):
    tokens, width = queries.shape
    cost = tokens * (ROWS + 2 * RADIUS)
    spec = lambda shape: pl.BlockSpec(shape, lambda i, *_: (0,) * (len(shape) - 1) + (i + pairs[0],))
    return pl.pallas_call(
        functools.partial(window_kernel, pairs[0]),
        grid_spec=pltpu.PrefetchScalarGridSpec(
            num_scalar_prefetch=2,
            grid=(pairs[1] - pairs[0],),
            in_specs=[
                spec((tokens, PAIR)),
                spec((2, tokens, PAIR)),
                spec((2, RADIUS, PAIR)),
                spec((2, RADIUS, PAIR)),
                pl.BlockSpec((tokens, 2), lambda i, *_: (0, 0)),
            ]
            + [pl.BlockSpec(memory_space=pl.ANY)] * len(done),
            out_specs=[spec((tokens, PAIR))] * 2,
            scratch_shapes=[
                pltpu.VMEM((tokens + 2 * RADIUS, PAIR), jnp.bfloat16),
                pltpu.VMEM((2, tokens + 2 * RADIUS, PAIR), jnp.bfloat16),
                pltpu.VMEM((2, ROWS, PAIR), jnp.float32),
                pltpu.VMEM((2, ROWS, PAIR), jnp.float32),
            ],
        ),
        out_shape=[jax.ShapeDtypeStruct((tokens, width), jnp.float32)] * 2,
        input_output_aliases={7 + i: i for i in range(len(done))},
        compiler_params=pltpu.CompilerParams(vmem_limit_bytes=VMEM),
        cost_estimate=pl.CostEstimate(
            flops=16 * cost * PAIR * (pairs[1] - pairs[0]),
            bytes_accessed=20 * tokens * PAIR * (pairs[1] - pairs[0]),
            transcendentals=2 * cost * (pairs[1] - pairs[0]),
        ),
        name="window_attention",
    )(radius, limits.reshape(-1), queries, keys_values, left, right, limits.T, *done)


def final_kernel(q_ref, pack_ref, part_ref, lse_ref, out_ref):
    keys = pack_ref[0]
    values = [with_ones(pack_ref[1], h) for h in range(2)]
    for r in range(0, q_ref.shape[0], ROWS):
        rows = pl.ds(r, ROWS)
        q = q_ref[rows, :]
        tops, accs = [], []
        for h in range(2):
            top, acc = softmax_dot(dot_t(only_head(q, h), keys), values[h])
            tops.append(top)
            accs.append(acc)
        summed, total, top = merge_heads(tops, accs)
        other = lse_ref[rows, :]
        highest = jnp.maximum(top, other)
        mine = jnp.exp2(top - highest)
        theirs = jnp.exp2(other - highest)
        out_ref[rows, :] = (
            (summed * mine + part_ref[rows, :] * theirs) / (total * mine + theirs)
        ).astype(jnp.bfloat16)


def final_attention(queries, pack_kv, part, lse):
    tokens, width = queries.shape
    spec = pl.BlockSpec((tokens, PAIR), lambda i: (0, i))
    return pl.pallas_call(
        final_kernel,
        grid=(width // PAIR,),
        in_specs=[spec, pl.BlockSpec((2, PACK, PAIR), lambda i: (0, 0, i)), spec, spec],
        out_specs=spec,
        out_shape=jax.ShapeDtypeStruct((tokens, width), jnp.bfloat16),
        compiler_params=pltpu.CompilerParams(vmem_limit_bytes=VMEM),
        cost_estimate=pl.CostEstimate(
            flops=16 * tokens * PACK * width,
            bytes_accessed=12 * tokens * width,
            transcendentals=tokens * PACK * width // HEAD_DIM,
        ),
        name="final_attention",
    )(queries, pack_kv, part, lse)


def project_kernel(order_ref, part_ref, proj_ref, out_ref, acc):
    step = pl.program_id(0)

    @pl.when(step == 0)
    def _():
        acc[...] = jnp.zeros_like(acc)

    for which in range(2):
        acc[which] += jnp.dot(part_ref[0], proj_ref[which], preferred_element_type=jnp.float32)

    @pl.when(step == pl.num_programs(0) - 1)
    def _():
        out_ref[...] = acc[...].astype(jnp.bfloat16)


def project(order, parts, pack_proj):
    count, rows, width = parts.shape
    columns = pack_proj.shape[2]
    return pl.pallas_call(
        project_kernel,
        grid_spec=pltpu.PrefetchScalarGridSpec(
            num_scalar_prefetch=1,
            grid=(count,),
            in_specs=[
                pl.BlockSpec((1, rows, width), lambda i, order: (i, 0, 0)),
                pl.BlockSpec((2, width, columns), lambda i, order: (0, order[i], 0)),
            ],
            out_specs=pl.BlockSpec((2, rows, columns), lambda i, order: (0, 0, 0)),
            scratch_shapes=[pltpu.VMEM((2, rows, columns), jnp.float32)],
        ),
        out_shape=jax.ShapeDtypeStruct((2, rows, columns), jnp.bfloat16),
        compiler_params=pltpu.CompilerParams(vmem_limit_bytes=VMEM),
        name="project",
    )(order, parts, pack_proj)


def shifted(x, axis, count, shift):
    return lax.ppermute(x, axis, [(i, (i + shift) % count) for i in range(count)])


def shards(queries, keys_values, pack_pos, bounds, radius, pack_proj):
    tokens, width = queries.shape
    heads = radius.shape[0]
    count = lax.axis_size("seq")
    share = PACK // count
    me = lax.axis_index("seq")
    first_pos = me * tokens

    ahead = (me + jnp.arange(count, dtype=jnp.int32)) % count
    local = pack_pos.reshape(count, share)[ahead].reshape(-1) - first_pos
    selector = (local[:, None] == jnp.arange(tokens, dtype=jnp.int32)[None, :]).astype(jnp.bfloat16)
    picked = jnp.dot(selector, queries, preferred_element_type=jnp.float32).astype(jnp.bfloat16)
    picked = picked.reshape(count, share, width)
    mine = picked[0]
    for s in range(1, count):
        mine = mine + shifted(picked[s], "seq", count, s)
    pack_query = jnp.concatenate([mine] + [shifted(mine, "seq", count, s) for s in range(1, count)])

    ends = count - 1
    left = lax.ppermute(
        keys_values[:, tokens - RADIUS :], "seq", [(i, i + 1) for i in range(ends)]
    )
    right = lax.ppermute(keys_values[:, :RADIUS], "seq", [(i + 1, i) for i in range(ends)])

    limits = bounds - (first_pos - RADIUS)
    pairs = width // PAIR
    edges = [0, pairs - pairs // 2, pairs - pairs // 4, pairs]
    window = ()

    def windowed(stage, after, beside):
        nonlocal window
        if edges[stage] == edges[stage + 1]:
            return beside
        held, _ = lax.optimization_barrier((radius, after))
        window = window_attention(
            queries, keys_values, left, right, limits, held, edges[stage : stage + 2], window
        )
        *window, beside = lax.optimization_barrier((*window, beside))
        return beside

    part, lse = pack_attention(pack_query, keys_values)
    part = part.reshape(count, share, width)
    lse = lse[:, ::HEAD_DIM].reshape(count, share, heads)
    parts, lses = [part[0]], [lse[0]]
    for s in range(1, count):
        parts.append(shifted(part[count - s], "seq", count, s))
        lses.append(shifted(lse[count - s], "seq", count, s))
    parts, lses = windowed(0, part, (parts, lses))
    lses = jnp.stack(lses)
    weights = jnp.exp2(lses - jnp.max(lses, axis=0, keepdims=True))
    weights = weights / jnp.sum(weights, axis=0, keepdims=True)
    packed = sum(
        parts[j].astype(jnp.float32).reshape(share, heads, HEAD_DIM) * weights[j][:, :, None]
        for j in range(count)
    )
    packed = packed.reshape(share, width).astype(jnp.bfloat16)

    axes = ("head", "rep")
    sides = lax.axis_size("head") * lax.axis_size("rep")
    here = lax.axis_index("head") * lax.axis_size("rep") + lax.axis_index("rep")
    gathered = [packed] + [shifted(packed, axes, sides, s) for s in range(1, sides)]
    gathered = jnp.stack(windowed(1, packed, gathered))
    order = (here - jnp.arange(sides, dtype=jnp.int32)) % sides
    pack_share = project(order, gathered, pack_proj)
    shares = [pack_share] + [shifted(pack_share, "seq", count, s) for s in range(1, count)]
    pack_kv = jnp.concatenate(windowed(2, pack_share, shares), axis=1)
    return final_attention(queries, pack_kv, *window)


def solution(mesh):
    return jax.shard_map(
        shards,
        mesh=mesh,
        in_specs=(
            P(("groups", "seq"), ("head", "rep")),
            P(None, ("groups", "seq"), ("head", "rep")),
            P("groups"),
            P(None, ("groups", "seq")),
            P(("head", "rep")),
            P(None, None, ("head", "rep")),
        ),
        out_specs=P(("groups", "seq"), ("head", "rep")),
        check_vma=False,
    )
```

```python
import functools
import math

import jax
import jax.numpy as jnp
from jax import lax
from jax.experimental import pallas as pl
from jax.experimental.pallas import tpu as pltpu
from jax.sharding import PartitionSpec as P

HEAD_DIM = 64
PACK = 512
RADIUS = 512
PAIR = 2 * HEAD_DIM
ROWS = 256
LOG2E = 1.4426950408889634
FACTOR = LOG2E / math.sqrt(HEAD_DIM)
LOW = -1e30
VMEM = 48 * 1024 * 1024


def lane_half(rows):
    return lax.broadcasted_iota(jnp.int32, (rows, PAIR), 1) // HEAD_DIM


def dot_t(a, b):
    return lax.dot_general(a, b, (((1,), (1,)), ((), ())), preferred_element_type=jnp.float32)


def only_head(x, h):
    return jnp.where(lane_half(x.shape[0]) == h, x, jnp.zeros_like(x))


def with_ones(x, h):
    return jnp.where(lane_half(x.shape[0]) == h, x, jnp.ones_like(x))


def softmax_dot(scores, values):
    top = jnp.max(scores, axis=1, keepdims=True)
    weights = jnp.exp2((scores - top) * FACTOR)
    acc = jnp.dot(weights.astype(jnp.bfloat16), values, preferred_element_type=jnp.float32)
    return top * FACTOR, acc


def merge_heads(tops, accs):
    half = lane_half(accs[0].shape[0])
    summed = jnp.where(half == 0, accs[0], accs[1])
    total = pltpu.roll(jnp.where(half == 0, accs[1], accs[0]), HEAD_DIM, 1)
    top = jnp.where(half == 0, tops[0], tops[1])
    return summed, total, top


def pack_kernel(kv_ref, *refs):
    *shares, out_ref, lse_ref, queries = refs
    pair = pl.program_id(0)
    for j, ref in enumerate(shares):
        queries[pl.ds(j * ref.shape[0], ref.shape[0]), :] = ref[...]
    keys = kv_ref[0]
    values = [with_ones(kv_ref[1], h) for h in range(2)]
    for r in range(0, queries.shape[0], ROWS):
        rows = pl.ds(r, ROWS)
        q = queries[rows, :]
        tops, accs = [], []
        for h in range(2):
            top, acc = softmax_dot(dot_t(only_head(q, h), keys), values[h])
            tops.append(top)
            accs.append(acc)
        summed, total, top = merge_heads(tops, accs)
        out_ref[rows, :] = (summed / total).astype(jnp.bfloat16)
        lse = top + jnp.log2(total)
        lane = lax.broadcasted_iota(jnp.int32, (ROWS, 128), 1)
        for h in range(2):
            column = lse[:, h * HEAD_DIM : h * HEAD_DIM + 1]
            lse_ref[rows, :] = jnp.where(lane == 2 * pair + h, column, lse_ref[rows, :])


def pack_attention(shares, keys_values):
    share, width = shares[0].shape
    rows = share * len(shares)
    tokens = keys_values.shape[1]
    return pl.pallas_call(
        pack_kernel,
        grid=(width // PAIR,),
        in_specs=[pl.BlockSpec((2, tokens, PAIR), lambda i: (0, 0, i))]
        + [pl.BlockSpec((share, PAIR), lambda i: (0, i))] * len(shares),
        out_specs=[
            pl.BlockSpec((rows, PAIR), lambda i: (0, i)),
            pl.BlockSpec((rows, 128), lambda i: (0, 0)),
        ],
        out_shape=[
            jax.ShapeDtypeStruct((rows, width), jnp.bfloat16),
            jax.ShapeDtypeStruct((rows, 128), jnp.float32),
        ],
        scratch_shapes=[pltpu.VMEM((rows, PAIR), jnp.bfloat16)],
        compiler_params=pltpu.CompilerParams(vmem_limit_bytes=VMEM),
        cost_estimate=pl.CostEstimate(
            flops=16 * rows * tokens * width,
            bytes_accessed=4 * tokens * width + 8 * rows * width,
            transcendentals=rows * tokens * width // HEAD_DIM,
        ),
        name="pack_attention",
    )(keys_values, *shares)


def combine_kernel(count, *refs):
    parts, lses, out_ref = refs[:count], refs[count:-1], refs[-1]
    rows, width = out_ref.shape
    held = [ref[...] for ref in lses]
    highest = functools.reduce(jnp.maximum, held)
    weights = [jnp.exp2(x - highest) for x in held]
    total = sum(weights)
    weights = [w / total for w in weights]
    half = lane_half(rows)
    for pair in range(width // PAIR):
        columns = pl.ds(pair * PAIR, PAIR)
        summed = jnp.zeros((rows, PAIR), jnp.float32)
        for ref, w in zip(parts, weights):
            one, two = (w[:, 2 * pair + h : 2 * pair + h + 1] for h in range(2))
            summed += ref[:, columns].astype(jnp.float32) * jnp.where(half == 0, one, two)
        out_ref[:, columns] = summed.astype(jnp.bfloat16)


def combine(parts, lses):
    return pl.pallas_call(
        functools.partial(combine_kernel, len(parts)),
        out_shape=jax.ShapeDtypeStruct(parts[0].shape, jnp.bfloat16),
        name="combine",
    )(*parts, *lses)


def window_kernel(
    first_pair, radius_ref, bounds_ref, q_ref, own_ref, left_ref, right_ref, limits_ref, *rest
):
    out_ref, lse_ref, keys, values, accs, tops = rest[-6:]
    tokens = q_ref.shape[0]
    pair = first_pair + pl.program_id(0)
    for at, ref in ((0, left_ref), (RADIUS, own_ref), (RADIUS + tokens, right_ref)):
        span = pl.ds(at, ref.shape[1])
        keys[span, :] = ref[0]
        for h in range(2):
            values[h, span, :] = with_ones(ref[1], h)

    def block(b, carry):
        first = pl.multiple_of(b * ROWS, ROWS)
        rows = pl.ds(first, ROWS)
        q = q_ref[rows, :]
        position = first + RADIUS + lax.broadcasted_iota(jnp.int32, (ROWS, 1), 0)
        lower = limits_ref[rows, 0:1]
        upper = limits_ref[rows, 1:2]
        for h in range(2):
            radius = radius_ref[2 * pair + h]
            low = jnp.maximum(lower, position - radius)
            high = jnp.minimum(upper, position + radius + 1)
            start = jnp.maximum(bounds_ref[first], first + RADIUS - radius)
            start = jnp.maximum(start, 0) // 128 * 128
            end = jnp.minimum(bounds_ref[tokens + first + ROWS - 1], first + RADIUS + ROWS + radius)
            need = end - start
            masked_q = only_head(q, h)

            def body(width):
                at = pl.multiple_of(jnp.minimum(start, tokens + 2 * RADIUS - width), 128)
                scores = dot_t(masked_q, keys[pl.ds(at, width), :])
                spot = lax.broadcasted_iota(jnp.int32, (ROWS, width), 1)
                allowed = (spot >= low - at) & (spot < high - at)
                top, acc = softmax_dot(
                    jnp.where(allowed, scores, LOW), values[h, pl.ds(at, width), :]
                )
                accs[h] = acc
                tops[h] = jnp.broadcast_to(top, (ROWS, PAIR))

            widest = ROWS + 2 * RADIUS
            widths = [w for w in (512, 640, 768, 896, 1024, 1152) if w < widest] + [widest]
            for index, width in enumerate(widths):
                fits = need <= width if width < widest else need > widths[index - 1]
                if 0 < index and width < widest:
                    fits = fits & (need > widths[index - 1])
                pl.when(fits)(functools.partial(body, width))
        summed, total, top = merge_heads([tops[0], tops[1]], [accs[0], accs[1]])
        out_ref[rows, :] = summed / total
        lse_ref[rows, :] = top + jnp.log2(total)
        return carry

    lax.fori_loop(0, tokens // ROWS, block, 0)


def window_attention(queries, keys_values, left, right, limits, radius, pairs, done):
    tokens, width = queries.shape
    cost = tokens * (ROWS + 2 * RADIUS)
    spec = lambda shape: pl.BlockSpec(shape, lambda i, *_: (0,) * (len(shape) - 1) + (i + pairs[0],))
    return pl.pallas_call(
        functools.partial(window_kernel, pairs[0]),
        grid_spec=pltpu.PrefetchScalarGridSpec(
            num_scalar_prefetch=2,
            grid=(pairs[1] - pairs[0],),
            in_specs=[
                spec((tokens, PAIR)),
                spec((2, tokens, PAIR)),
                spec((2, RADIUS, PAIR)),
                spec((2, RADIUS, PAIR)),
                pl.BlockSpec((tokens, 2), lambda i, *_: (0, 0)),
            ]
            + [pl.BlockSpec(memory_space=pl.ANY)] * len(done),
            out_specs=[spec((tokens, PAIR))] * 2,
            scratch_shapes=[
                pltpu.VMEM((tokens + 2 * RADIUS, PAIR), jnp.bfloat16),
                pltpu.VMEM((2, tokens + 2 * RADIUS, PAIR), jnp.bfloat16),
                pltpu.VMEM((2, ROWS, PAIR), jnp.float32),
                pltpu.VMEM((2, ROWS, PAIR), jnp.float32),
            ],
        ),
        out_shape=[jax.ShapeDtypeStruct((tokens, width), jnp.float32)] * 2,
        input_output_aliases={7 + i: i for i in range(len(done))},
        compiler_params=pltpu.CompilerParams(vmem_limit_bytes=VMEM),
        cost_estimate=pl.CostEstimate(
            flops=16 * cost * PAIR * (pairs[1] - pairs[0]),
            bytes_accessed=20 * tokens * PAIR * (pairs[1] - pairs[0]),
            transcendentals=2 * cost * (pairs[1] - pairs[0]),
        ),
        name="window_attention",
    )(radius, limits.reshape(-1), queries, keys_values, left, right, limits.T, *done)


def final_kernel(q_ref, part_ref, lse_ref, *refs):
    *shares, out_ref, pack = refs
    for j, ref in enumerate(shares):
        pack[:, pl.ds(j * ref.shape[1], ref.shape[1]), :] = ref[...]
    keys = pack[0]
    values = [with_ones(pack[1], h) for h in range(2)]
    for r in range(0, q_ref.shape[0], ROWS):
        rows = pl.ds(r, ROWS)
        q = q_ref[rows, :]
        tops, accs = [], []
        for h in range(2):
            top, acc = softmax_dot(dot_t(only_head(q, h), keys), values[h])
            tops.append(top)
            accs.append(acc)
        summed, total, top = merge_heads(tops, accs)
        other = lse_ref[rows, :]
        highest = jnp.maximum(top, other)
        mine = jnp.exp2(top - highest)
        theirs = jnp.exp2(other - highest)
        out_ref[rows, :] = (
            (summed * mine + part_ref[rows, :] * theirs) / (total * mine + theirs)
        ).astype(jnp.bfloat16)


def final_attention(queries, shares, part, lse):
    tokens, width = queries.shape
    spec = pl.BlockSpec((tokens, PAIR), lambda i: (0, i))
    return pl.pallas_call(
        final_kernel,
        grid=(width // PAIR,),
        in_specs=[spec] * 3
        + [pl.BlockSpec((2, x.shape[1], PAIR), lambda i: (0, 0, i)) for x in shares],
        out_specs=spec,
        scratch_shapes=[pltpu.VMEM((2, PACK, PAIR), jnp.bfloat16)],
        out_shape=jax.ShapeDtypeStruct((tokens, width), jnp.bfloat16),
        compiler_params=pltpu.CompilerParams(vmem_limit_bytes=VMEM),
        cost_estimate=pl.CostEstimate(
            flops=16 * tokens * PACK * width,
            bytes_accessed=12 * tokens * width,
            transcendentals=tokens * PACK * width // HEAD_DIM,
        ),
        name="final_attention",
    )(queries, part, lse, *shares)


def project_kernel(order_ref, part_ref, proj_ref, out_ref, acc):
    step = pl.program_id(0)

    @pl.when(step == 0)
    def _():
        acc[...] = jnp.zeros_like(acc)

    for which in range(2):
        acc[which] += jnp.dot(part_ref[0], proj_ref[which], preferred_element_type=jnp.float32)

    @pl.when(step == pl.num_programs(0) - 1)
    def _():
        out_ref[...] = acc[...].astype(jnp.bfloat16)


def project(order, parts, pack_proj):
    count, rows, width = parts.shape
    columns = pack_proj.shape[2]
    return pl.pallas_call(
        project_kernel,
        grid_spec=pltpu.PrefetchScalarGridSpec(
            num_scalar_prefetch=1,
            grid=(count,),
            in_specs=[
                pl.BlockSpec((1, rows, width), lambda i, order: (i, 0, 0)),
                pl.BlockSpec((2, width, columns), lambda i, order: (0, order[i], 0)),
            ],
            out_specs=pl.BlockSpec((2, rows, columns), lambda i, order: (0, 0, 0)),
            scratch_shapes=[pltpu.VMEM((2, rows, columns), jnp.float32)],
        ),
        out_shape=jax.ShapeDtypeStruct((2, rows, columns), jnp.bfloat16),
        compiler_params=pltpu.CompilerParams(vmem_limit_bytes=VMEM),
        name="project",
    )(order, parts, pack_proj)


def shifted(x, axis, count, shift):
    return lax.ppermute(x, axis, [(i, (i + shift) % count) for i in range(count)])


def shards(queries, keys_values, pack_pos, bounds, radius, pack_proj):
    tokens, width = queries.shape
    count = lax.axis_size("seq")
    share = PACK // count
    me = lax.axis_index("seq")
    first_pos = me * tokens

    ahead = (me + jnp.arange(count, dtype=jnp.int32)) % count
    local = pack_pos.reshape(count, share)[ahead].reshape(-1) - first_pos
    selector = (local[:, None] == jnp.arange(tokens, dtype=jnp.int32)[None, :]).astype(jnp.bfloat16)
    picked = jnp.dot(selector, queries, preferred_element_type=jnp.float32).astype(jnp.bfloat16)
    picked = picked.reshape(count, share, width)
    mine = picked[0]
    for s in range(1, count):
        mine = mine + shifted(picked[s], "seq", count, s)
    pack_query = [mine] + [shifted(mine, "seq", count, s) for s in range(1, count)]

    ends = count - 1
    tail, head = keys_values[:, tokens - RADIUS :], keys_values[:, :RADIUS]
    pack_query, tail, head = lax.optimization_barrier((pack_query, tail, head))
    left = lax.ppermute(tail, "seq", [(i, i + 1) for i in range(ends)])
    right = lax.ppermute(head, "seq", [(i + 1, i) for i in range(ends)])

    limits = bounds - (first_pos - RADIUS)
    pairs = width // PAIR
    edges = [0, pairs // 4, pairs // 2, pairs]
    window = ()

    def windowed(stage, after, beside):
        nonlocal window
        if edges[stage] == edges[stage + 1]:
            return beside
        held, _ = lax.optimization_barrier((radius, after))
        window = window_attention(
            queries, keys_values, left, right, limits, held, edges[stage : stage + 2], window
        )
        *window, beside = lax.optimization_barrier((*window, beside))
        return beside

    part, lse = pack_attention(pack_query, keys_values)
    part = part.reshape(count, share, width)
    lse = lse.reshape(count, share, 128)
    parts, lses = [part[0]], [lse[0]]
    for s in range(1, count):
        parts.append(shifted(part[count - s], "seq", count, s))
        lses.append(shifted(lse[count - s], "seq", count, s))
    parts, lses = windowed(0, part, (parts, lses))
    packed = combine(parts, lses)

    axes = ("head", "rep")
    sides = lax.axis_size("head") * lax.axis_size("rep")
    here = lax.axis_index("head") * lax.axis_size("rep") + lax.axis_index("rep")
    gathered = [packed] + [shifted(packed, axes, sides, s) for s in range(1, sides)]
    gathered = jnp.stack(windowed(1, packed, gathered))
    order = (here - jnp.arange(sides, dtype=jnp.int32)) % sides
    pack_share = project(order, gathered, pack_proj)
    shares = [pack_share] + [shifted(pack_share, "seq", count, s) for s in range(1, count)]
    shares = windowed(2, pack_share, shares)
    return final_attention(queries, shares, *window)


def solution(mesh):
    return jax.shard_map(
        shards,
        mesh=mesh,
        in_specs=(
            P(("groups", "seq"), ("head", "rep")),
            P(None, ("groups", "seq"), ("head", "rep")),
            P("groups"),
            P(None, ("groups", "seq")),
            P(("head", "rep")),
            P(None, None, ("head", "rep")),
        ),
        out_specs=P(("groups", "seq"), ("head", "rep")),
        check_vma=False,
    )
```

```python
import functools
import math

import jax
import jax.numpy as jnp
from jax import lax
from jax.experimental import pallas as pl
from jax.experimental.pallas import tpu as pltpu
from jax.sharding import PartitionSpec as P

HEAD_DIM = 64
PACK = 512
RADIUS = 512
PAIR = 2 * HEAD_DIM
ROWS = 256
LOG2E = 1.4426950408889634
FACTOR = LOG2E / math.sqrt(HEAD_DIM)
LOW = -1e30
VMEM = 48 * 1024 * 1024


def lane_half(rows):
    return lax.broadcasted_iota(jnp.int32, (rows, PAIR), 1) // HEAD_DIM


def dot_t(a, b):
    return lax.dot_general(a, b, (((1,), (1,)), ((), ())), preferred_element_type=jnp.float32)


def only_head(x, h):
    return jnp.where(lane_half(x.shape[0]) == h, x, jnp.zeros_like(x))


def with_ones(x, h):
    return jnp.where(lane_half(x.shape[0]) == h, x, jnp.ones_like(x))


def softmax_dot(scores, values):
    top = jnp.max(scores, axis=1, keepdims=True)
    weights = jnp.exp2((scores - top) * FACTOR)
    acc = jnp.dot(weights.astype(jnp.bfloat16), values, preferred_element_type=jnp.float32)
    return top * FACTOR, acc


def merge_heads(tops, accs):
    half = lane_half(accs[0].shape[0])
    summed = jnp.where(half == 0, accs[0], accs[1])
    total = pltpu.roll(jnp.where(half == 0, accs[1], accs[0]), HEAD_DIM, 1)
    top = jnp.where(half == 0, tops[0], tops[1])
    return summed, total, top


def pack_kernel(kv_ref, *refs):
    *shares, out_ref, queries, lse_ref = refs
    pair = pl.program_id(0)
    columns = pl.ds(pl.multiple_of(pair * PAIR, PAIR), PAIR)
    for j, ref in enumerate(shares):
        queries[pl.ds(j * ref.shape[0], ref.shape[0]), :] = ref[...]
    keys = kv_ref[0]
    values = [with_ones(kv_ref[1], h) for h in range(2)]
    for r in range(0, queries.shape[0], ROWS):
        rows = pl.ds(r, ROWS)
        q = queries[rows, :]
        tops, accs = [], []
        for h in range(2):
            top, acc = softmax_dot(dot_t(only_head(q, h), keys), values[h])
            tops.append(top)
            accs.append(acc)
        summed, total, top = merge_heads(tops, accs)
        out_ref[rows, columns] = (summed / total).astype(jnp.bfloat16)
        lse = top + jnp.log2(total)
        lane = lax.broadcasted_iota(jnp.int32, (ROWS, 128), 1)
        for h in range(2):
            column = lse[:, h * HEAD_DIM : h * HEAD_DIM + 1]
            lse_ref[rows, :] = jnp.where(lane == 2 * pair + h, column, lse_ref[rows, :])

    @pl.when(pair == pl.num_programs(0) - 1)
    def _():
        lse = lse_ref[...]
        high = lse.astype(jnp.bfloat16).astype(jnp.float32)
        middle = (lse - high).astype(jnp.bfloat16).astype(jnp.float32)
        low = lse - high - middle
        lane = lax.broadcasted_iota(jnp.int32, lse.shape, 1)
        terms = jnp.where(lane < 64, pltpu.roll(middle, 32, 1), pltpu.roll(low, 64, 1))
        terms = jnp.where(lane < 32, high, terms)
        out_ref[:, out_ref.shape[1] - 128 :] = terms.astype(jnp.bfloat16)


def pack_attention(shares, keys_values):
    share, width = shares[0].shape
    rows = share * len(shares)
    tokens = keys_values.shape[1]
    return pl.pallas_call(
        pack_kernel,
        grid=(width // PAIR,),
        in_specs=[pl.BlockSpec((2, tokens, PAIR), lambda i: (0, 0, i))]
        + [pl.BlockSpec((share, PAIR), lambda i: (0, i))] * len(shares),
        out_specs=pl.BlockSpec((rows, width + 128), lambda i: (0, 0)),
        out_shape=jax.ShapeDtypeStruct((rows, width + 128), jnp.bfloat16),
        scratch_shapes=[
            pltpu.VMEM((rows, PAIR), jnp.bfloat16),
            pltpu.VMEM((rows, 128), jnp.float32),
        ],
        compiler_params=pltpu.CompilerParams(vmem_limit_bytes=VMEM),
        cost_estimate=pl.CostEstimate(
            flops=16 * rows * tokens * width,
            bytes_accessed=4 * tokens * width + 8 * rows * width,
            transcendentals=rows * tokens * width // HEAD_DIM,
        ),
        name="pack_attention",
    )(keys_values, *shares)


def combine_kernel(*refs):
    *parts, out_ref = refs
    rows, width = out_ref.shape
    held = [ref[:, width:].astype(jnp.float32) for ref in parts]
    held = [x + pltpu.roll(x, 96, 1) + pltpu.roll(x, 64, 1) for x in held]
    highest = functools.reduce(jnp.maximum, held)
    weights = [jnp.exp2(x - highest) for x in held]
    total = sum(weights)
    weights = [w / total for w in weights]
    half = lane_half(rows)
    for pair in range(width // PAIR):
        columns = pl.ds(pair * PAIR, PAIR)
        summed = jnp.zeros((rows, PAIR), jnp.float32)
        for ref, w in zip(parts, weights):
            one, two = (w[:, 2 * pair + h : 2 * pair + h + 1] for h in range(2))
            summed += ref[:, columns].astype(jnp.float32) * jnp.where(half == 0, one, two)
        out_ref[:, columns] = summed.astype(jnp.bfloat16)


def combine(parts):
    rows, width = parts[0].shape
    return pl.pallas_call(
        combine_kernel,
        out_shape=jax.ShapeDtypeStruct((rows, width - 128), jnp.bfloat16),
        name="combine",
    )(*parts)


def window_kernel(
    first_pair, radius_ref, bounds_ref, q_ref, own_ref, left_ref, right_ref, limits_ref, *rest
):
    out_ref, lse_ref, keys, values, accs, tops = rest[-6:]
    tokens = q_ref.shape[0]
    pair = first_pair + pl.program_id(0)
    for at, ref in ((0, left_ref), (RADIUS, own_ref), (RADIUS + tokens, right_ref)):
        span = pl.ds(at, ref.shape[1])
        keys[span, :] = ref[0]
        for h in range(2):
            values[h, span, :] = with_ones(ref[1], h)

    def block(b, carry):
        first = pl.multiple_of(b * ROWS, ROWS)
        rows = pl.ds(first, ROWS)
        q = q_ref[rows, :]
        position = first + RADIUS + lax.broadcasted_iota(jnp.int32, (ROWS, 1), 0)
        lower = limits_ref[rows, 0:1]
        upper = limits_ref[rows, 1:2]
        for h in range(2):
            radius = radius_ref[2 * pair + h]
            low = jnp.maximum(lower, position - radius)
            high = jnp.minimum(upper, position + radius + 1)
            start = jnp.maximum(bounds_ref[first], first + RADIUS - radius)
            start = jnp.maximum(start, 0) // 128 * 128
            end = jnp.minimum(bounds_ref[tokens + first + ROWS - 1], first + RADIUS + ROWS + radius)
            need = end - start
            masked_q = only_head(q, h)

            def body(width):
                at = pl.multiple_of(jnp.minimum(start, tokens + 2 * RADIUS - width), 128)
                scores = dot_t(masked_q, keys[pl.ds(at, width), :])
                spot = lax.broadcasted_iota(jnp.int32, (ROWS, width), 1)
                allowed = (spot >= low - at) & (spot < high - at)
                top, acc = softmax_dot(
                    jnp.where(allowed, scores, LOW), values[h, pl.ds(at, width), :]
                )
                accs[h] = acc
                tops[h] = jnp.broadcast_to(top, (ROWS, PAIR))

            widest = ROWS + 2 * RADIUS
            widths = [w for w in (512, 640, 768, 896, 1024, 1152) if w < widest] + [widest]
            for index, width in enumerate(widths):
                fits = need <= width if width < widest else need > widths[index - 1]
                if 0 < index and width < widest:
                    fits = fits & (need > widths[index - 1])
                pl.when(fits)(functools.partial(body, width))
        summed, total, top = merge_heads([tops[0], tops[1]], [accs[0], accs[1]])
        out_ref[rows, :] = summed / total
        lse_ref[rows, :] = top + jnp.log2(total)
        return carry

    lax.fori_loop(0, tokens // ROWS, block, 0)


def window_attention(queries, keys_values, left, right, limits, radius, pairs, done):
    tokens, width = queries.shape
    cost = tokens * (ROWS + 2 * RADIUS)
    spec = lambda shape: pl.BlockSpec(shape, lambda i, *_: (0,) * (len(shape) - 1) + (i + pairs[0],))
    return pl.pallas_call(
        functools.partial(window_kernel, pairs[0]),
        grid_spec=pltpu.PrefetchScalarGridSpec(
            num_scalar_prefetch=2,
            grid=(pairs[1] - pairs[0],),
            in_specs=[
                spec((tokens, PAIR)),
                spec((2, tokens, PAIR)),
                spec((2, RADIUS, PAIR)),
                spec((2, RADIUS, PAIR)),
                pl.BlockSpec((tokens, 2), lambda i, *_: (0, 0)),
            ]
            + [pl.BlockSpec(memory_space=pl.ANY)] * len(done),
            out_specs=[spec((tokens, PAIR))] * 2,
            scratch_shapes=[
                pltpu.VMEM((tokens + 2 * RADIUS, PAIR), jnp.bfloat16),
                pltpu.VMEM((2, tokens + 2 * RADIUS, PAIR), jnp.bfloat16),
                pltpu.VMEM((2, ROWS, PAIR), jnp.float32),
                pltpu.VMEM((2, ROWS, PAIR), jnp.float32),
            ],
        ),
        out_shape=[jax.ShapeDtypeStruct((tokens, width), jnp.float32)] * 2,
        input_output_aliases={7 + i: i for i in range(len(done))},
        compiler_params=pltpu.CompilerParams(vmem_limit_bytes=VMEM),
        cost_estimate=pl.CostEstimate(
            flops=16 * cost * PAIR * (pairs[1] - pairs[0]),
            bytes_accessed=20 * tokens * PAIR * (pairs[1] - pairs[0]),
            transcendentals=2 * cost * (pairs[1] - pairs[0]),
        ),
        name="window_attention",
    )(radius, limits.reshape(-1), queries, keys_values, left, right, limits.T, *done)


def final_kernel(q_ref, part_ref, lse_ref, *refs):
    *shares, out_ref, pack = refs
    for j, ref in enumerate(shares):
        pack[:, pl.ds(j * ref.shape[1], ref.shape[1]), :] = ref[...]
    keys = pack[0]
    values = [with_ones(pack[1], h) for h in range(2)]
    for r in range(0, q_ref.shape[0], ROWS):
        rows = pl.ds(r, ROWS)
        q = q_ref[rows, :]
        tops, accs = [], []
        for h in range(2):
            top, acc = softmax_dot(dot_t(only_head(q, h), keys), values[h])
            tops.append(top)
            accs.append(acc)
        summed, total, top = merge_heads(tops, accs)
        other = lse_ref[rows, :]
        highest = jnp.maximum(top, other)
        mine = jnp.exp2(top - highest)
        theirs = jnp.exp2(other - highest)
        out_ref[rows, :] = (
            (summed * mine + part_ref[rows, :] * theirs) / (total * mine + theirs)
        ).astype(jnp.bfloat16)


def final_attention(queries, shares, part, lse):
    tokens, width = queries.shape
    spec = pl.BlockSpec((tokens, PAIR), lambda i: (0, i))
    return pl.pallas_call(
        final_kernel,
        grid=(width // PAIR,),
        in_specs=[spec] * 3
        + [pl.BlockSpec((2, x.shape[1], PAIR), lambda i: (0, 0, i)) for x in shares],
        out_specs=spec,
        scratch_shapes=[pltpu.VMEM((2, PACK, PAIR), jnp.bfloat16)],
        out_shape=jax.ShapeDtypeStruct((tokens, width), jnp.bfloat16),
        compiler_params=pltpu.CompilerParams(vmem_limit_bytes=VMEM),
        cost_estimate=pl.CostEstimate(
            flops=16 * tokens * PACK * width,
            bytes_accessed=12 * tokens * width,
            transcendentals=tokens * PACK * width // HEAD_DIM,
        ),
        name="final_attention",
    )(queries, part, lse, *shares)


def project_kernel(order_ref, part_ref, proj_ref, out_ref, acc):
    step = pl.program_id(0)

    @pl.when(step == 0)
    def _():
        acc[...] = jnp.zeros_like(acc)

    for which in range(2):
        acc[which] += jnp.dot(part_ref[0], proj_ref[which], preferred_element_type=jnp.float32)

    @pl.when(step == pl.num_programs(0) - 1)
    def _():
        out_ref[...] = acc[...].astype(jnp.bfloat16)


def project(order, parts, pack_proj):
    count, rows, width = parts.shape
    columns = pack_proj.shape[2]
    return pl.pallas_call(
        project_kernel,
        grid_spec=pltpu.PrefetchScalarGridSpec(
            num_scalar_prefetch=1,
            grid=(count,),
            in_specs=[
                pl.BlockSpec((1, rows, width), lambda i, order: (i, 0, 0)),
                pl.BlockSpec((2, width, columns), lambda i, order: (0, order[i], 0)),
            ],
            out_specs=pl.BlockSpec((2, rows, columns), lambda i, order: (0, 0, 0)),
            scratch_shapes=[pltpu.VMEM((2, rows, columns), jnp.float32)],
        ),
        out_shape=jax.ShapeDtypeStruct((2, rows, columns), jnp.bfloat16),
        compiler_params=pltpu.CompilerParams(vmem_limit_bytes=VMEM),
        name="project",
    )(order, parts, pack_proj)


def shifted(x, axis, count, shift):
    return lax.ppermute(x, axis, [(i, (i + shift) % count) for i in range(count)])


def shards(queries, keys_values, pack_pos, bounds, radius, pack_proj):
    tokens, width = queries.shape
    count = lax.axis_size("seq")
    share = PACK // count
    me = lax.axis_index("seq")
    first_pos = me * tokens

    ahead = (me + jnp.arange(count, dtype=jnp.int32)) % count
    local = pack_pos.reshape(count, share)[ahead].reshape(-1) - first_pos
    selector = (local[:, None] == jnp.arange(tokens, dtype=jnp.int32)[None, :]).astype(jnp.bfloat16)
    picked = jnp.dot(selector, queries, preferred_element_type=jnp.float32).astype(jnp.bfloat16)
    picked = picked.reshape(count, share, width)
    mine = picked[0]
    for s in range(1, count):
        mine = mine + shifted(picked[s], "seq", count, s)
    pack_query = [mine] + [shifted(mine, "seq", count, s) for s in range(1, count)]

    ends = count - 1
    tail, head = keys_values[:, tokens - RADIUS :], keys_values[:, :RADIUS]
    pack_query, tail, head = lax.optimization_barrier((pack_query, tail, head))
    left = lax.ppermute(tail, "seq", [(i, i + 1) for i in range(ends)])
    right = lax.ppermute(head, "seq", [(i + 1, i) for i in range(ends)])

    limits = bounds - (first_pos - RADIUS)
    pairs = width // PAIR
    edges = [0, 0, pairs // 4, pairs]
    window = ()

    def windowed(stage, after, beside):
        nonlocal window
        if edges[stage] == edges[stage + 1]:
            return beside
        held, _ = lax.optimization_barrier((radius, after))
        window = window_attention(
            queries, keys_values, left, right, limits, held, edges[stage : stage + 2], window
        )
        *window, beside = lax.optimization_barrier((*window, beside))
        return beside

    part = pack_attention(pack_query, keys_values).reshape(count, share, width + 128)
    parts = [part[0]] + [shifted(part[count - s], "seq", count, s) for s in range(1, count)]
    packed = combine(windowed(0, part, parts))

    axes = ("head", "rep")
    sides = lax.axis_size("head") * lax.axis_size("rep")
    here = lax.axis_index("head") * lax.axis_size("rep") + lax.axis_index("rep")
    gathered = [packed] + [shifted(packed, axes, sides, s) for s in range(1, sides)]
    gathered = jnp.stack(windowed(1, packed, gathered))
    order = (here - jnp.arange(sides, dtype=jnp.int32)) % sides
    pack_share = project(order, gathered, pack_proj)
    shares = [pack_share] + [shifted(pack_share, "seq", count, s) for s in range(1, count)]
    shares = windowed(2, pack_share, shares)
    return final_attention(queries, shares, *window)


def solution(mesh):
    return jax.shard_map(
        shards,
        mesh=mesh,
        in_specs=(
            P(("groups", "seq"), ("head", "rep")),
            P(None, ("groups", "seq"), ("head", "rep")),
            P("groups"),
            P(None, ("groups", "seq")),
            P(("head", "rep")),
            P(None, None, ("head", "rep")),
        ),
        out_specs=P(("groups", "seq"), ("head", "rep")),
        check_vma=False,
    )
```

```python
import functools
import math

import jax
import jax.numpy as jnp
from jax import lax
from jax.experimental import pallas as pl
from jax.experimental.pallas import tpu as pltpu
from jax.sharding import PartitionSpec as P

HEAD_DIM = 64
PACK = 512
RADIUS = 512
PAIR = 2 * HEAD_DIM
ROWS = 256
LOG2E = 1.4426950408889634
FACTOR = LOG2E / math.sqrt(HEAD_DIM)
LOW = -1e30
VMEM = 48 * 1024 * 1024


def lane_half(rows):
    return lax.broadcasted_iota(jnp.int32, (rows, PAIR), 1) // HEAD_DIM


def dot_t(a, b):
    return lax.dot_general(a, b, (((1,), (1,)), ((), ())), preferred_element_type=jnp.float32)


def only_head(x, h):
    return jnp.where(lane_half(x.shape[0]) == h, x, jnp.zeros_like(x))


def with_ones(x, h):
    return jnp.where(lane_half(x.shape[0]) == h, x, jnp.ones_like(x))


def softmax_dot(scores, values):
    top = jnp.max(scores, axis=1, keepdims=True)
    weights = jnp.exp2((scores - top) * FACTOR)
    acc = jnp.dot(weights.astype(jnp.bfloat16), values, preferred_element_type=jnp.float32)
    return top * FACTOR, acc


def merge_heads(tops, accs):
    half = lane_half(accs[0].shape[0])
    summed = jnp.where(half == 0, accs[0], accs[1])
    total = pltpu.roll(jnp.where(half == 0, accs[1], accs[0]), HEAD_DIM, 1)
    top = jnp.where(half == 0, tops[0], tops[1])
    return summed, total, top


def pack_kernel(kv_ref, *refs):
    *shares, out_ref, queries, lse_ref = refs
    pair = pl.program_id(0)
    columns = pl.ds(pl.multiple_of(pair * PAIR, PAIR), PAIR)
    for j, ref in enumerate(shares):
        queries[pl.ds(j * ref.shape[0], ref.shape[0]), :] = ref[...]
    keys = kv_ref[0]
    values = [with_ones(kv_ref[1], h) for h in range(2)]
    for r in range(0, queries.shape[0], ROWS):
        rows = pl.ds(r, ROWS)
        q = queries[rows, :]
        tops, accs = [], []
        for h in range(2):
            top, acc = softmax_dot(dot_t(only_head(q, h), keys), values[h])
            tops.append(top)
            accs.append(acc)
        summed, total, top = merge_heads(tops, accs)
        out_ref[rows, columns] = (summed / total).astype(jnp.bfloat16)
        lse = top + jnp.log2(total)
        lane = lax.broadcasted_iota(jnp.int32, (ROWS, 128), 1)
        for h in range(2):
            column = lse[:, h * HEAD_DIM : h * HEAD_DIM + 1]
            lse_ref[rows, :] = jnp.where(lane == 2 * pair + h, column, lse_ref[rows, :])

    @pl.when(pair == pl.num_programs(0) - 1)
    def _():
        lse = lse_ref[...]
        high = lse.astype(jnp.bfloat16).astype(jnp.float32)
        middle = (lse - high).astype(jnp.bfloat16).astype(jnp.float32)
        low = lse - high - middle
        lane = lax.broadcasted_iota(jnp.int32, lse.shape, 1)
        terms = jnp.where(lane < 64, pltpu.roll(middle, 32, 1), pltpu.roll(low, 64, 1))
        terms = jnp.where(lane < 32, high, terms)
        out_ref[:, out_ref.shape[1] - 128 :] = terms.astype(jnp.bfloat16)


def pack_attention(shares, keys_values):
    share, width = shares[0].shape
    rows = share * len(shares)
    tokens = keys_values.shape[1]
    return pl.pallas_call(
        pack_kernel,
        grid=(width // PAIR,),
        in_specs=[pl.BlockSpec((2, tokens, PAIR), lambda i: (0, 0, i))]
        + [pl.BlockSpec((share, PAIR), lambda i: (0, i))] * len(shares),
        out_specs=pl.BlockSpec((rows, width + 128), lambda i: (0, 0)),
        out_shape=jax.ShapeDtypeStruct((rows, width + 128), jnp.bfloat16),
        scratch_shapes=[
            pltpu.VMEM((rows, PAIR), jnp.bfloat16),
            pltpu.VMEM((rows, 128), jnp.float32),
        ],
        compiler_params=pltpu.CompilerParams(vmem_limit_bytes=VMEM),
        cost_estimate=pl.CostEstimate(
            flops=16 * rows * tokens * width,
            bytes_accessed=4 * tokens * width + 8 * rows * width,
            transcendentals=rows * tokens * width // HEAD_DIM,
        ),
        name="pack_attention",
    )(keys_values, *shares)


def combine_kernel(*refs):
    *parts, out_ref = refs
    rows, width = out_ref.shape
    held = [ref[:, width:].astype(jnp.float32) for ref in parts]
    held = [x + pltpu.roll(x, 96, 1) + pltpu.roll(x, 64, 1) for x in held]
    highest = functools.reduce(jnp.maximum, held)
    weights = [jnp.exp2(x - highest) for x in held]
    total = sum(weights)
    weights = [w / total for w in weights]
    half = lane_half(rows)
    for pair in range(width // PAIR):
        columns = pl.ds(pair * PAIR, PAIR)
        summed = jnp.zeros((rows, PAIR), jnp.float32)
        for ref, w in zip(parts, weights):
            one, two = (w[:, 2 * pair + h : 2 * pair + h + 1] for h in range(2))
            summed += ref[:, columns].astype(jnp.float32) * jnp.where(half == 0, one, two)
        out_ref[:, columns] = summed.astype(jnp.bfloat16)


def combine(parts):
    rows, width = parts[0].shape
    return pl.pallas_call(
        combine_kernel,
        out_shape=jax.ShapeDtypeStruct((rows, width - 128), jnp.bfloat16),
        name="combine",
    )(*parts)


def window_kernel(
    first_pair, radius_ref, bounds_ref, q_ref, own_ref, left_ref, right_ref, limits_ref, *rest
):
    out_ref, lse_ref, keys, values, accs, tops = rest[-6:]
    tokens = q_ref.shape[0]
    pair = first_pair + pl.program_id(0)
    for at, ref in ((0, left_ref), (RADIUS, own_ref), (RADIUS + tokens, right_ref)):
        span = pl.ds(at, ref.shape[1])
        keys[span, :] = ref[0]
        for h in range(2):
            values[h, span, :] = with_ones(ref[1], h)

    def block(b, carry):
        first = pl.multiple_of(b * ROWS, ROWS)
        rows = pl.ds(first, ROWS)
        q = q_ref[rows, :]
        position = first + RADIUS + lax.broadcasted_iota(jnp.int32, (ROWS, 1), 0)
        lower = limits_ref[rows, 0:1]
        upper = limits_ref[rows, 1:2]
        for h in range(2):
            radius = radius_ref[2 * pair + h]
            low = jnp.maximum(lower, position - radius)
            high = jnp.minimum(upper, position + radius + 1)
            start = jnp.maximum(bounds_ref[first], first + RADIUS - radius)
            start = jnp.maximum(start, 0) // 128 * 128
            end = jnp.minimum(bounds_ref[tokens + first + ROWS - 1], first + RADIUS + ROWS + radius)
            need = end - start
            masked_q = only_head(q, h)

            def body(width):
                at = pl.multiple_of(jnp.minimum(start, tokens + 2 * RADIUS - width), 128)
                scores = dot_t(masked_q, keys[pl.ds(at, width), :])
                spot = lax.broadcasted_iota(jnp.int32, (ROWS, width), 1)
                allowed = (spot >= low - at) & (spot < high - at)
                top, acc = softmax_dot(
                    jnp.where(allowed, scores, LOW), values[h, pl.ds(at, width), :]
                )
                accs[h] = acc
                tops[h] = jnp.broadcast_to(top, (ROWS, PAIR))

            widest = ROWS + 2 * RADIUS
            widths = [w for w in (512, 640, 768, 896, 1024, 1152) if w < widest] + [widest]
            for index, width in enumerate(widths):
                fits = need <= width if width < widest else need > widths[index - 1]
                if 0 < index and width < widest:
                    fits = fits & (need > widths[index - 1])
                pl.when(fits)(functools.partial(body, width))
        summed, total, top = merge_heads([tops[0], tops[1]], [accs[0], accs[1]])
        out_ref[rows, :] = summed / total
        lse_ref[rows, :] = top + jnp.log2(total)
        return carry

    lax.fori_loop(0, tokens // ROWS, block, 0)


def window_attention(queries, keys_values, left, right, limits, radius, pairs, done):
    tokens, width = queries.shape
    cost = tokens * (ROWS + 2 * RADIUS)
    spec = lambda shape: pl.BlockSpec(shape, lambda i, *_: (0,) * (len(shape) - 1) + (i + pairs[0],))
    return pl.pallas_call(
        functools.partial(window_kernel, pairs[0]),
        grid_spec=pltpu.PrefetchScalarGridSpec(
            num_scalar_prefetch=2,
            grid=(pairs[1] - pairs[0],),
            in_specs=[
                spec((tokens, PAIR)),
                spec((2, tokens, PAIR)),
                pl.BlockSpec((2, RADIUS, PAIR), lambda i, *_: (0, 0, i)),
                pl.BlockSpec((2, RADIUS, PAIR), lambda i, *_: (0, 0, i)),
                pl.BlockSpec((tokens, 2), lambda i, *_: (0, 0)),
            ]
            + [pl.BlockSpec(memory_space=pl.ANY)] * len(done),
            out_specs=[spec((tokens, PAIR))] * 2,
            scratch_shapes=[
                pltpu.VMEM((tokens + 2 * RADIUS, PAIR), jnp.bfloat16),
                pltpu.VMEM((2, tokens + 2 * RADIUS, PAIR), jnp.bfloat16),
                pltpu.VMEM((2, ROWS, PAIR), jnp.float32),
                pltpu.VMEM((2, ROWS, PAIR), jnp.float32),
            ],
        ),
        out_shape=[jax.ShapeDtypeStruct((tokens, width), jnp.float32)] * 2,
        input_output_aliases={7 + i: i for i in range(len(done))},
        compiler_params=pltpu.CompilerParams(vmem_limit_bytes=VMEM),
        cost_estimate=pl.CostEstimate(
            flops=16 * cost * PAIR * (pairs[1] - pairs[0]),
            bytes_accessed=20 * tokens * PAIR * (pairs[1] - pairs[0]),
            transcendentals=2 * cost * (pairs[1] - pairs[0]),
        ),
        name="window_attention",
    )(radius, limits.reshape(-1), queries, keys_values, left, right, limits.T, *done)


def final_kernel(q_ref, part_ref, lse_ref, *refs):
    *shares, out_ref, pack = refs
    for j, ref in enumerate(shares):
        pack[:, pl.ds(j * ref.shape[1], ref.shape[1]), :] = ref[...]
    keys = pack[0]
    values = [with_ones(pack[1], h) for h in range(2)]
    for r in range(0, q_ref.shape[0], ROWS):
        rows = pl.ds(r, ROWS)
        q = q_ref[rows, :]
        tops, accs = [], []
        for h in range(2):
            top, acc = softmax_dot(dot_t(only_head(q, h), keys), values[h])
            tops.append(top)
            accs.append(acc)
        summed, total, top = merge_heads(tops, accs)
        other = lse_ref[rows, :]
        highest = jnp.maximum(top, other)
        mine = jnp.exp2(top - highest)
        theirs = jnp.exp2(other - highest)
        out_ref[rows, :] = (
            (summed * mine + part_ref[rows, :] * theirs) / (total * mine + theirs)
        ).astype(jnp.bfloat16)


def final_attention(queries, shares, part, lse):
    tokens, width = queries.shape
    spec = pl.BlockSpec((tokens, PAIR), lambda i: (0, i))
    return pl.pallas_call(
        final_kernel,
        grid=(width // PAIR,),
        in_specs=[spec] * 3
        + [pl.BlockSpec((2, x.shape[1], PAIR), lambda i: (0, 0, i)) for x in shares],
        out_specs=spec,
        scratch_shapes=[pltpu.VMEM((2, PACK, PAIR), jnp.bfloat16)],
        out_shape=jax.ShapeDtypeStruct((tokens, width), jnp.bfloat16),
        compiler_params=pltpu.CompilerParams(vmem_limit_bytes=VMEM),
        cost_estimate=pl.CostEstimate(
            flops=16 * tokens * PACK * width,
            bytes_accessed=12 * tokens * width,
            transcendentals=tokens * PACK * width // HEAD_DIM,
        ),
        name="final_attention",
    )(queries, part, lse, *shares)


def project_kernel(order_ref, part_ref, proj_ref, out_ref, acc):
    step = pl.program_id(0)

    @pl.when(step == 0)
    def _():
        acc[...] = jnp.zeros_like(acc)

    for which in range(2):
        acc[which] += jnp.dot(part_ref[0], proj_ref[which], preferred_element_type=jnp.float32)

    @pl.when(step == pl.num_programs(0) - 1)
    def _():
        out_ref[...] = acc[...].astype(jnp.bfloat16)


def project(order, parts, pack_proj):
    count, rows, width = parts.shape
    columns = pack_proj.shape[2]
    return pl.pallas_call(
        project_kernel,
        grid_spec=pltpu.PrefetchScalarGridSpec(
            num_scalar_prefetch=1,
            grid=(count,),
            in_specs=[
                pl.BlockSpec((1, rows, width), lambda i, order: (i, 0, 0)),
                pl.BlockSpec((2, width, columns), lambda i, order: (0, order[i], 0)),
            ],
            out_specs=pl.BlockSpec((2, rows, columns), lambda i, order: (0, 0, 0)),
            scratch_shapes=[pltpu.VMEM((2, rows, columns), jnp.float32)],
        ),
        out_shape=jax.ShapeDtypeStruct((2, rows, columns), jnp.bfloat16),
        compiler_params=pltpu.CompilerParams(vmem_limit_bytes=VMEM),
        name="project",
    )(order, parts, pack_proj)


def shifted(x, axis, count, shift):
    return lax.ppermute(x, axis, [(i, (i + shift) % count) for i in range(count)])


def shards(queries, keys_values, pack_pos, bounds, radius, pack_proj):
    tokens, width = queries.shape
    count = lax.axis_size("seq")
    share = PACK // count
    me = lax.axis_index("seq")
    first_pos = me * tokens

    ahead = (me + jnp.arange(count, dtype=jnp.int32)) % count
    local = pack_pos.reshape(count, share)[ahead].reshape(-1) - first_pos
    selector = (local[:, None] == jnp.arange(tokens, dtype=jnp.int32)[None, :]).astype(jnp.bfloat16)
    picked = jnp.dot(selector, queries, preferred_element_type=jnp.float32).astype(jnp.bfloat16)
    picked = picked.reshape(count, share, width)
    mine = picked[0]
    for s in range(1, count):
        mine = mine + shifted(picked[s], "seq", count, s)
    pack_query = [mine] + [shifted(mine, "seq", count, s) for s in range(1, count)]

    limits = bounds - (first_pos - RADIUS)
    pairs = width // PAIR
    edges = [0, 0, pairs // 4, pairs]
    window = ()

    def halos(stage, after):
        columns = slice(edges[stage] * PAIR, edges[stage + 1] * PAIR)
        tail, head = keys_values[:, tokens - RADIUS :, columns], keys_values[:, :RADIUS, columns]
        if tail.shape[2] == 0:
            return (), after
        after, tail, head = lax.optimization_barrier((after, tail, head))
        ends = count - 1
        left = lax.ppermute(tail, "seq", [(i, i + 1) for i in range(ends)])
        right = lax.ppermute(head, "seq", [(i + 1, i) for i in range(ends)])
        return (left, right), after

    def windowed(stage, after, beside, sides):
        nonlocal window
        if edges[stage] == edges[stage + 1]:
            return beside
        held, _ = lax.optimization_barrier((radius, after))
        window = window_attention(
            queries, keys_values, *sides, limits, held, edges[stage : stage + 2], window
        )
        *window, beside = lax.optimization_barrier((*window, beside))
        return beside

    early, pack_query = halos(1, pack_query)
    part = pack_attention(pack_query, keys_values).reshape(count, share, width + 128)
    parts = [part[0]] + [shifted(part[count - s], "seq", count, s) for s in range(1, count)]
    early, parts = lax.optimization_barrier((early, parts))
    late, packed = halos(2, combine(parts))

    axes = ("head", "rep")
    sides = lax.axis_size("head") * lax.axis_size("rep")
    here = lax.axis_index("head") * lax.axis_size("rep") + lax.axis_index("rep")
    gathered = [packed] + [shifted(packed, axes, sides, s) for s in range(1, sides)]
    gathered = jnp.stack(windowed(1, packed, gathered, early))
    order = (here - jnp.arange(sides, dtype=jnp.int32)) % sides
    pack_share = project(order, gathered, pack_proj)
    shares = [pack_share] + [shifted(pack_share, "seq", count, s) for s in range(1, count)]
    shares = windowed(2, pack_share, shares, late)
    return final_attention(queries, shares, *window)


def solution(mesh):
    return jax.shard_map(
        shards,
        mesh=mesh,
        in_specs=(
            P(("groups", "seq"), ("head", "rep")),
            P(None, ("groups", "seq"), ("head", "rep")),
            P("groups"),
            P(None, ("groups", "seq")),
            P(("head", "rep")),
            P(None, None, ("head", "rep")),
        ),
        out_specs=P(("groups", "seq"), ("head", "rep")),
        check_vma=False,
    )
```
